128 devices in a mesh: grp: 4 (over x), shard: 32 (over z, y, core).
Axes of the slice: x: 4, y: 4, z: 4, core: 2. Of those that a mesh axis runs over, the one named last changes fastest.
Arguments:
- grads: bfloat16 [4, 32, 8192, 1024], P('grp', 'shard'), may hold values from -6 to 6
- momentum: float32 [4, 8192, 1024], P('grp', 'shard'), may hold values from -18 to 18
- positions: int32 [4, 128, 16, 32], P('grp', 'shard'), may hold values from 0 to 4095, as said below
- counts: int32 [4], P('grp'), may hold values from 4 to 32, as said below
Outputs:
- new_momentum: float32 [4, 8192, 1024], P('grp', 'shard')
- update: float32 [8192, 1024], P('shard')
The draws below stay inside these ranges and needn't reach their ends.
Inputs may be any that keep to these rules, and one draw needn't show every extreme that they name: Within each block of each group the 32 positions are distinct. Each group uses the first counts[g] positions of every block; in every draw one group uses all 32.
All inputs are finite; a program needn't handle non-finite values.
Results may differ from the reference program's by a relative error of at most 0.0003.
Values sent between devices are 32-bit elements; how exact they have to be, the bound alone decides.
No kernel may reach another device: no remote copies, remote signals or barrier semaphores. Data moves between devices by JAX's collectives and lax.ppermute only.
A program may use at most 256 MiB of HBM per device.

```python
import jax
import jax.numpy as jnp
from jax import lax

D = 8192
COLS = 1024
SPAN = 64
TOPK = 32
N_GRP = 4
N_SHARD = 32


def draw_positions(key, part):
    key = jax.random.fold_in(key, 11)
    shape = (N_GRP, D // SPAN, COLS // SPAN, SPAN * SPAN)
    scores = jax.random.randint(key, shape, 0, 2 ** 18)
    scores = scores * (SPAN * SPAN) + lax.broadcasted_iota(jnp.int32, shape, 3)
    unused, picked = lax.top_k(scores, TOPK)
    return picked.astype(jnp.int32)


def draw_counts(key, part):
    key = jax.random.fold_in(key, 23)
    first_key, second_key = jax.random.split(key)
    base = jax.random.randint(first_key, (N_GRP,), max(1, TOPK // 8), TOPK // 2 + 1)
    chosen = jax.random.randint(second_key, (), 0, N_GRP)
    return jnp.where(jnp.arange(N_GRP) == chosen, TOPK, base).astype(jnp.int32)


def raised(entries, stream_key, source, target, blocks, factor):
    def block_of(dim):
        return (jnp.arange(entries.shape[dim]) // (entries.shape[dim] // blocks)).reshape((-1,) + (1,) * (entries.ndim - 1 - dim))

    one_side = jax.random.permutation(stream_key, blocks)[block_of(target)]
    far = (block_of(target) + blocks // 2) % blocks
    return jnp.where((block_of(source) == one_side) | (block_of(source) == far), factor * entries, entries)


def block_scale(own_key, extent, pieces, least, top_value):
    factor_of = 1.0
    for dim, shards_of in pieces:
        heights = jax.random.uniform(jax.random.fold_in(jax.random.fold_in(own_key, 6), dim), (shards_of,), jnp.float32, least / len(pieces), top_value / len(pieces))
        factor_of = factor_of * jnp.repeat(jnp.exp(heights), extent[dim] // shards_of).reshape((-1,) + (1,) * (len(extent) - 1 - dim))
    return factor_of


def bell_draw(own_key, extent, spread, bound, cuts=(), dtype=jnp.bfloat16):
    drawn = spread * jax.random.normal(own_key, extent, jnp.float32)
    if cuts:
        drawn = drawn * block_scale(own_key, extent, cuts, -0.22, 0.18)
    return jnp.clip(drawn, -bound, bound).astype(dtype)


def bell_draw_with(key, extent, spread, limit, shards, heavy, dtype=jnp.bfloat16):
    values = spread * jax.random.normal(key, extent, jnp.float32)
    if shards:
        values = values * block_scale(key, extent, shards, -0.22, 0.18)
    return jnp.clip(raised(values, jax.random.fold_in(key, 3), *heavy), -limit, limit).astype(dtype)


def setup_inputs(seed: int = 0) -> dict:
    splits = jax.random.split(jax.random.key(seed), 5)
    return {
        "grads": bell_draw_with(splits[0], (N_GRP, N_SHARD, D, COLS), 1.0, 6.0, ((0, 4), (1, 32)), (1, 2, 32, 2.75)),
        "momentum": bell_draw(splits[1], (N_GRP, D, COLS), 3.0, 18.0, ((0, 4), (1, 32)), jnp.float32),
        "positions": draw_positions(jax.random.fold_in(splits[4], 71), 0),
        "counts": draw_counts(jax.random.fold_in(splits[4], 71), 0),
    }


momentum_decay = 0.999

def dct_basis(tile_width):
    frequency = lax.broadcasted_iota(jnp.int32, (tile_width, tile_width), 0).astype(jnp.float32)
    position = lax.broadcasted_iota(jnp.int32, (tile_width, tile_width), 1).astype(jnp.float32)
    norming = jnp.where(frequency == 0, jnp.sqrt(1.0 / tile_width), jnp.sqrt(2.0 / tile_width))
    return norming * jnp.cos(jnp.pi * (2.0 * position + 1.0) * frequency / (2.0 * tile_width))

def to_coefficients(field, basis):
    tile_width = basis.shape[0]
    height, across = field.shape
    tiles = field.reshape(height // tile_width, tile_width, across // tile_width, tile_width)
    result = jnp.einsum('km,amcn,ln->akcl', basis, tiles, basis, precision=lax.Precision.HIGHEST)
    return result.reshape(height, across)

def tile_major(coeffs, tile_width):
    height, across = coeffs.shape
    tiles = coeffs.reshape(height // tile_width, tile_width, across // tile_width, tile_width)
    return tiles.transpose(0, 2, 1, 3).reshape(height // tile_width, across // tile_width, tile_width * tile_width)

def to_field(coeffs, basis):
    tile_width = basis.shape[0]
    blocks_down, blocks_across, squared = coeffs.shape
    tiles = coeffs.reshape(blocks_down, blocks_across, tile_width, tile_width)
    result = jnp.einsum('km,abkl,ln->ambn', basis, tiles, basis, precision=lax.Precision.HIGHEST)
    return result.reshape(blocks_down * tile_width, blocks_across * tile_width)

def scatter_into(values, places, target_shape):
    blocks_down, blocks_across, squared = target_shape
    down_index = jnp.arange(blocks_down).astype(jnp.int32).reshape(blocks_down, 1, 1)
    across_index = jnp.arange(blocks_across).astype(jnp.int32).reshape(1, blocks_across, 1)
    return jnp.zeros(target_shape, jnp.float32).at[down_index, across_index, places].add(values)

def reference(grads, momentum, positions, counts):
    basis = dct_basis(SPAN)
    zero_field = jnp.zeros((D, COLS), jnp.float32)

    def accumulate(running, piece):
        return (running + piece.astype(jnp.float32), None)
    fields = []
    owned = []
    for group_index in range(N_GRP):
        summed, unused = lax.scan(accumulate, zero_field, grads[group_index])
        updated = momentum_decay * momentum[group_index] + summed
        coeffs = tile_major(to_coefficients(updated, basis), SPAN)
        places = positions[group_index]
        live_mask = jnp.arange(TOPK).astype(jnp.int32).reshape(1, 1, TOPK) < counts[group_index]
        values = jnp.where(live_mask, jnp.take_along_axis(coeffs, places, axis=2), 0.0)
        own_coeffs = scatter_into(values, places, coeffs.shape)
        fields.append(updated - to_field(own_coeffs, basis))
        owned.append(own_coeffs)
    combined = owned[0]
    for extra in owned[1:]:
        combined = combined + extra
    update = to_field(combined / N_GRP, basis)
    return (jnp.stack(fields), update)
```

```python
import functools

import jax
import jax.numpy as jnp
import numpy as np
from jax import lax
from jax.experimental import pallas as pl
from jax.experimental.pallas import tpu as pltpu
from jax.sharding import PartitionSpec as P

SPAN = 64
DECAY = 0.999
NZ, NY, NC, NX = 4, 4, 2, 4
ROWS, COLS = 256, 1024
HW = COLS // 2
TOPK = 32
NA, NT, TILE = ROWS // SPAN, 4, 256
PARTS = ((0, 128), (128, 128))
OFFSETS = ((2, 2), (1, -1), (-1, 1), (0, 0))
F32, BF16 = jnp.float32, jnp.bfloat16


def vm(shape, dtype=F32):
    return pltpu.VMEM(shape, dtype)


VSPEC = pl.BlockSpec(memory_space=pltpu.VMEM)
ASPEC = pl.BlockSpec(memory_space=pl.ANY)


def position():
    s = lax.axis_index("shard")
    return lax.axis_index("grp"), s // (NY * NC), (s // NC) % NY, s % NC


def axes(other=False):
    _, z, y, c = position()
    c = 1 - c if other else c
    return c, jnp.where(c == 0, z, y), jnp.where(c == 0, y, z)


def fetch(g_ref, buf, sems, stage, r0, rows, other):
    core, first, _ = axes(other)
    copies = []
    for h in range(2):
        mine = (first + (OFFSETS[stage][h] + 4)) % 4
        for s in range(4):
            zi, yi = jnp.where(core == 0, mine, s), jnp.where(core == 0, s, mine)
            src = g_ref.at[zi, yi, core, pl.ds(r0, rows), pl.ds(h * HW, HW)]
            cp = pltpu.make_async_copy(src, buf.at[h, s], sems.at[h, s])
            cp.start()
            copies.append(cp)
    return copies


def conv_kernel(stage, r0, rows, g_ref, w_ref, buf, sems):
    copies = fetch(g_ref, buf, sems, stage, r0, rows, True)
    for h in range(2):
        for s in range(4):
            copies[4 * h + s].wait()
            w_ref[h, s] = buf[h, s].astype(F32)


def sum_kernel(stage, r0, rows, n_in, g_ref, *refs):
    r_ref, refs = refs[0], refs[1:]
    ins, outs, (buf, sems) = refs[: 2 * n_in], refs[2 * n_in : 2 * n_in + 2], refs[-2:]
    copies = fetch(g_ref, buf, sems, stage, r0, rows, False)
    for h in range(2):
        for s in range(4):
            copies[4 * h + s].wait()
            total = buf[h, s].astype(F32) + r_ref[h, s]
            for m in range(n_in):
                total = total + ins[2 * m + h][s]
            outs[h][s] = total


def turn_kernel(r0, rows, g_ref, r_ref, *refs):
    ins, outs, (buf, sems) = refs[:4], refs[4:12], refs[-2:]
    copies = fetch(g_ref, buf, sems, 3, r0, rows, False)
    _, _, here = axes()
    for cp in copies:
        cp.wait()
    for h in range(2):
        for stage in range(4):
            s = (here + (OFFSETS[stage][h] + 4)) % 4
            outs[2 * stage + h][...] = (
                buf[h, s].astype(F32) + r_ref[h, s] + ins[h][s] + ins[2 + h][s]
            )


def relay_kernel(*refs):
    for h in range(2):
        refs[4 + h][...] = refs[h][...] + refs[2 + h][...]


def call(body, outs, args, name, scratch=(), limit=8, cost=(1_000_000, 4_000_000), onto=None):
    space = {"v": pltpu.VMEM, "h": pltpu.HBM}
    spec = {"v": VSPEC, "h": ASPEC, "s": pl.BlockSpec(memory_space=pltpu.SMEM)}
    vals = [pltpu.with_memory_space_constraint(a, space[kind]) if kind in space else a for a, kind in args]
    in_specs = [spec[kind] for _, kind in args]
    whole = isinstance(outs, jax.ShapeDtypeStruct)
    aliases = {}
    if onto is not None:
        vals, in_specs, aliases = vals + [onto], in_specs + [ASPEC], {len(vals): 0}
    return pl.pallas_call(
        body,
        out_shape=outs,
        in_specs=in_specs,
        out_specs=ASPEC if whole else jax.tree.map(lambda o: VSPEC, outs, is_leaf=lambda o: not isinstance(o, (list, tuple))),
        scratch_shapes=list(scratch),
        input_output_aliases=aliases,
        compiler_params=pltpu.CompilerParams(vmem_limit_bytes=limit * 2**20),
        cost_estimate=pl.CostEstimate(flops=cost[0], bytes_accessed=cost[1], transcendentals=0),
        name=name,
    )(*vals)


def place(z, y, c):
    return (z % NZ * NY + y % NY) * NC + c % NC


def everywhere():
    return [(z, y, c) for z in range(NZ) for y in range(NY) for c in range(NC)]


def to_other_core(x):
    return lax.ppermute(x, "shard", [(place(z, y, c), place(z, y, c + 1)) for z, y, c in everywhere()])


def along(x, step, second=False):
    pairs = []
    for z, y, c in everywhere():
        to = (z + step, y, c) if (c == 0) != second else (z, y + step, c)
        pairs.append((place(z, y, c), place(*to)))
    return lax.ppermute(x, "shard", pairs)


def move_grp(x, d):
    return lax.ppermute(x, "grp", [(i, (i + d) % NX) for i in range(NX)])


WAY = ((-1, 1), (1, -1), (-1, 1))


def reduce_part(g, r0, rows):
    scratch = [pltpu.VMEM((2, 4, rows, HW), BF16), pltpu.SemaphoreType.DMA((2, 4))]
    chunk, small = (4, rows, HW), (rows, HW)
    got = []
    for stage in range(4):
        w = call(functools.partial(conv_kernel, stage, r0, rows), vm((2,) + chunk), [(g, "h")], f"conv{stage}", scratch)
        got.append(to_other_core(w))

    def summed(stage, ins):
        n_in = len(ins) // 2
        return call(
            functools.partial(sum_kernel, stage, r0, rows, n_in),
            [vm(chunk)] * 2,
            [(g, "h"), (got[stage], "v")] + [(x, "v") for x in ins],
            f"sum{stage}",
            scratch,
        )

    first = [along(x, WAY[0][h]) for h, x in enumerate(summed(0, []))]
    direct = [along(x, WAY[1][h]) for h, x in enumerate(summed(1, []))]
    relay = [along(x, WAY[2][h]) for h, x in enumerate(summed(2, first))]
    turned = call(
        functools.partial(turn_kernel, r0, rows),
        [vm(small)] * 8,
        [(g, "h"), (got[3], "v")] + [(x, "v") for x in direct + relay],
        "turn",
        scratch,
    )
    first = [along(x, WAY[0][h], True) for h, x in enumerate(turned[0:2])]
    direct = [along(x, WAY[1][h], True) for h, x in enumerate(turned[2:4])]
    on = call(relay_kernel, [vm(small)] * 2, [(x, "v") for x in list(turned[4:6]) + first], "relay")
    relay = [along(x, WAY[2][h], True) for h, x in enumerate(on)]
    return list(turned[6:8]), direct, relay


def split(x):
    high = x.astype(BF16)
    return high, (x - high.astype(F32)).astype(BF16)


def dot(a, b, last=False):
    return lax.dot_general(a, b, (((1,), (1 if last else 0,)), ((), ())), preferred_element_type=F32)


def dot3(x, high, low):
    xh, xl = split(x)
    n = x.shape[0]
    both = dot(jnp.concatenate([xh, xl], axis=0), high)
    return both[:n] + both[n:] + dot(xh, low)


def basis():
    k, n = np.arange(SPAN)[:, None], np.arange(SPAN)[None, :]
    q = np.sqrt(np.where(k == 0, 1.0, 2.0) / SPAN) * np.cos(np.pi * (2 * n + 1) * k / (2 * SPAN))
    return q, np.kron(np.eye(TILE // SPAN), q.T)


def halves_of(m):
    high = m.astype(np.float32).astype(jnp.bfloat16)
    low = (m - high.astype(np.float64)).astype(np.float32).astype(jnp.bfloat16)
    return [jnp.asarray(high), jnp.asarray(low)]


def prep_kernel(p0, p1, p2, p3, qh_ref, ql_ref, bt_ref, l_ref):
    me = position()[0]
    block = lax.broadcasted_iota(jnp.int32, (1, 128), 1) // TOPK
    for i, ref in enumerate((p0, p1, p2, p3)):
        lanes = pl.ds(pl.multiple_of(((me + (4 - i)) % NX) * 128, 128), 128)

        @pl.loop(0, NA)
        def _(a, ref=ref, lanes=lanes):
            for t in range(NT):
                pos = ref[a, t : t + 1, :]
                row, col = pos // SPAN, pos % SPAN + block * SPAN
                hit = lax.broadcasted_iota(jnp.int32, (TILE, 128), 0) == col
                bt_ref[a, t, :, lanes] = jnp.where(hit, 1.0, 0.0).astype(BF16)
                at = jnp.where(lax.broadcasted_iota(jnp.int32, (SPAN, 128), 0) == row, 1.0, 0.0).astype(BF16)
                l_ref[a, t, :, lanes] = dot(qh_ref[...], at) + dot(ql_ref[...], at)


def values_kernel(a0, na, m_ref, count_ref, dh_ref, dl_ref, bt_ref, l_ref, *refs):
    ins, (up_ref, v_ref) = refs[:6], refs[6:]
    me = position()[0]
    lanes = pl.ds(pl.multiple_of(me * 128, 128), 128)
    live = lax.broadcasted_iota(jnp.int32, (1, 128), 1) % TOPK < count_ref[0]
    for t in range(NT):
        h, cols, part = t // 2, pl.ds(t * TILE, TILE), pl.ds(t % 2 * TILE, TILE)
        up = DECAY * m_ref[a0 * SPAN : (a0 + na) * SPAN, cols] + (ins[h][:, part] + ins[2 + h][:, part] + ins[4 + h][:, part])
        up_ref[:, cols] = up
        zh, zl = split(dot3(up, dh_ref[...], dl_ref[...]))
        for a in range(na):
            rows = slice(a * SPAN, (a + 1) * SPAN)
            got = dot(jnp.concatenate([zh[rows], zl[rows]], axis=0), bt_ref[a0 + a, t, :, lanes])
            v = jnp.sum((got[:SPAN] + got[SPAN:]) * l_ref[a0 + a, t, :, lanes], axis=0, keepdims=True)
            v_ref[4 * a + t : 4 * a + t + 1, :] = jnp.where(live, v, 0.0)


def field(v, l, bt, eh, el):
    high, low = split(l * v)
    got = dot(jnp.concatenate([high, low], axis=0), bt, last=True)
    return dot3(got[:SPAN] + got[SPAN:], eh, el)


def store_rows(buf, out_ref, a0, na, sem):
    cp = pltpu.make_async_copy(buf, out_ref.at[pl.ds(a0 * SPAN, na * SPAN), :], sem)
    cp.start()
    cp.wait()


def keep_kernel(a0, na, up_ref, v_ref, eh_ref, el_ref, bt_ref, l_ref, *refs):
    out_ref, buf, sem = refs[-3:]
    lanes = pl.ds(pl.multiple_of(position()[0] * 128, 128), 128)
    for a in range(na):
        for t in range(NT):
            rows, cols = pl.ds(a * SPAN, SPAN), pl.ds(t * TILE, TILE)
            got = field(v_ref[4 * a + t : 4 * a + t + 1, :], l_ref[a0 + a, t, :, lanes], bt_ref[a0 + a, t, :, lanes], eh_ref[...], el_ref[...])
            buf[rows, cols] = up_ref[rows, cols] - got
    store_rows(buf, out_ref, a0, na, sem)


def update_kernel(a0, na, v0, v1, v2, v3, eh_ref, el_ref, bt_ref, l_ref, *refs):
    out_ref, buf, vals, sem = refs[-4:]
    me = position()[0]
    for i, ref in enumerate((v0, v1, v2, v3)):
        vals[:, pl.ds(pl.multiple_of(((me + (4 - i)) % NX) * 128, 128), 128)] = ref[...] * (1.0 / NX)
    for a in range(na):
        for t in range(NT):
            got = field(vals[4 * a + t : 4 * a + t + 1, :], l_ref[a0 + a, t], bt_ref[a0 + a, t], eh_ref[...], el_ref[...])
            buf[pl.ds(a * SPAN, SPAN), pl.ds(t * TILE, TILE)] = got
    store_rows(buf, out_ref, a0, na, sem)


def from_groups(x):
    return [x] + [move_grp(x, i) for i in (1, 2, 3)]


def per_device(grads, momentum, positions, counts):
    g = grads.reshape(NZ, NY, NC, ROWS, COLS)
    q, four = basis()
    dh, dl = halves_of(four)
    eh, el = halves_of(four.T)
    qh, ql = halves_of(q.T)
    places = from_groups(positions.reshape(NA, NT, 128))
    bt, l = call(
        prep_kernel,
        [vm((NA, NT, TILE, NX * 128), BF16), vm((NA, NT, SPAN, NX * 128))],
        [(x, "v") for x in places + [qh, ql]],
        "prep",
        limit=16,
        cost=(10_000_000, 20_000_000),
    )
    tables = [(bt, "v"), (l, "v")]
    kept = update = None
    for r0, rows in PARTS:
        a0, na = r0 // SPAN, rows // SPAN
        sums = reduce_part(g, r0, rows)
        up, v = call(
            functools.partial(values_kernel, a0, na),
            [vm((rows, COLS)), vm((NT * na, 128))],
            [(momentum[0], "v"), (counts, "s"), (dh, "v"), (dl, "v")] + tables + [(x, "v") for s in sums for x in s],
            "values",
        )
        vs = from_groups(v)
        scratch = [pltpu.VMEM((rows, COLS), F32), pltpu.SemaphoreType.DMA]
        kept = call(
            functools.partial(keep_kernel, a0, na),
            jax.ShapeDtypeStruct((ROWS, COLS), F32),
            [(up, "v"), (v, "v"), (eh, "v"), (el, "v")] + tables,
            "keep",
            scratch,
            onto=kept,
        )
        update = call(
            functools.partial(update_kernel, a0, na),
            jax.ShapeDtypeStruct((ROWS, COLS), F32),
            [(x, "v") for x in vs] + [(eh, "v"), (el, "v")] + tables,
            "update",
            [scratch[0], pltpu.VMEM((NT * na, NX * 128), F32), scratch[1]],
            onto=update,
        )
    return kept[None], update


def solution(mesh):
    in_specs = (
        P("grp", "shard", None, None),
        P("grp", "shard", None),
        P("grp", "shard", None, None),
        P("grp"),
    )
    out_specs = (P("grp", "shard", None), P("shard", None))
    return jax.shard_map(
        per_device, mesh=mesh, in_specs=in_specs, out_specs=out_specs, check_vma=False
    )
```

```python
import functools

import jax
import jax.numpy as jnp
import numpy as np
from jax import lax
from jax.experimental import pallas as pl
from jax.experimental.pallas import tpu as pltpu
from jax.sharding import PartitionSpec as P

SPAN = 64
DECAY = 0.999
NZ, NY, NC, NX = 4, 4, 2, 4
ROWS, COLS = 256, 1024
HW = COLS // 2
TOPK = 32
AHEAD = (200_000_000_000, 1_000_000_000)
SLOTS = 8
NA, NT, TILE = ROWS // SPAN, 4, 256
PARTS = ((0, 128), (128, 128))
OFFSETS = ((2, 2), (1, -1), (-1, 1), (0, 0))
F32, BF16 = jnp.float32, jnp.bfloat16


def vm(shape, dtype=F32):
    return pltpu.VMEM(shape, dtype)


VSPEC = pl.BlockSpec(memory_space=pltpu.VMEM)
ASPEC = pl.BlockSpec(memory_space=pl.ANY)


def position():
    s = lax.axis_index("shard")
    return lax.axis_index("grp"), s // (NY * NC), (s // NC) % NY, s % NC


def axes(other=False):
    _, z, y, c = position()
    c = 1 - c if other else c
    return c, jnp.where(c == 0, z, y), jnp.where(c == 0, y, z)


def fetch(g_ref, buf, sems, stage, r0, rows, other):
    core, first, _ = axes(other)
    copies = {}
    for h in range(2):
        mine = (first + (OFFSETS[stage][h] + 4)) % 4
        for s in range(4):
            z, y = jnp.where(core == 0, mine, s), jnp.where(core == 0, s, mine)
            src = g_ref.at[z, y, core, pl.ds(r0, rows), pl.ds(h * HW, HW)]
            copies[h, s] = pltpu.make_async_copy(src, buf.at[h, s], sems.at[h, s])
            copies[h, s].start()
    return copies


def conv_kernel(stages, r0, rows, g_ref, w_ref, buf, sems, wide, wide_sems):
    copies = [fetch(g_ref, buf.at[i], sems.at[i], stage, r0, rows, True) for i, stage in enumerate(stages)]
    out = []
    for i in range(len(stages)):
        for (h, s), cp in copies[i].items():
            cp.wait()
            slot = len(out) % SLOTS
            if len(out) >= SLOTS:
                out[-SLOTS].wait()
            wide[slot] = buf[i, h, s].astype(F32)
            out.append(pltpu.make_async_copy(wide.at[slot], w_ref.at[i, h, s], wide_sems.at[slot]))
            out[-1].start()
    for cp in out[-SLOTS:]:
        cp.wait()


def near_conv_kernel(stages, r0, rows, g_ref, w_ref, buf, sems):
    copies = [fetch(g_ref, buf.at[i], sems.at[i], stage, r0, rows, True) for i, stage in enumerate(stages)]
    for i in range(len(stages)):
        for (h, s), cp in copies[i].items():
            cp.wait()
            w_ref[i, h, s] = buf[i, h, s].astype(F32)


class Terms:
    def __init__(self, stage, r0, rows, g_ref, r_ref, at, messages, staging, near=False):
        (i, first_row), (own, other, more, sems) = at, staging
        self.own, self.other, self.more = own, r_ref.at[i] if near else other, None if messages is None else more
        self.copies = {key: [cp] for key, cp in fetch(g_ref, own, sems.at[0], stage, r0, rows, False).items()}
        for h, s in self.copies:
            src = r_ref.at[i, h, s, pl.ds(r0 - first_row, rows)]
            if not near:
                self.copies[h, s].append(pltpu.make_async_copy(src, other.at[h, s], sems.at[1, h, s]))
            if messages is not None:
                self.copies[h, s].append(pltpu.make_async_copy(messages[h].at[s], more.at[h, s], sems.at[2, h, s]))
            for cp in self.copies[h, s][1:]:
                cp.start()

    def get(self, h, s):
        for cp in self.copies[h, s]:
            cp.wait()
        total = self.own[h, s].astype(F32) + self.other[h, s]
        return total if self.more is None else total + self.more[h, s]


def send_kernel(at, r0, rows, g_ref, *refs):
    (*others, minus, plus), staging = refs[:-4], refs[-4:]
    near = len(others) == 2
    terms = [
        Terms(i, r0, rows, g_ref, others[i % len(others)], at[i], None, [ref.at[i] for ref in staging], near)
        for i in range(2)
    ]
    for i, to in enumerate(((minus, plus), (plus, minus))):
        for h in range(2):
            for s in range(4):
                to[h][i, s] = terms[i].get(h, s)


def pass_kernel(at, r0, rows, g_ref, r_ref, minus, plus, *refs):
    terms = Terms(2, r0, rows, g_ref, r_ref, at, (minus.at[0], plus.at[0]), refs[2:])
    for h in range(2):
        for s in range(4):
            refs[h][s] = terms.get(h, s)


def before_kernel(at, r0, rows, g_ref, r_ref, minus, plus, out_ref, *staging):
    terms = Terms(3, r0, rows, g_ref, r_ref, at, (plus.at[1], minus.at[1]), staging)
    for h in range(2):
        for s in range(4):
            out_ref[h, s] = terms.get(h, s)


def turn_kernel(sum_ref, relay0, relay1, *refs):
    (minus, plus), left, own = refs[0:2], refs[2:4], refs[4:6]
    to = ((minus.at[0], plus.at[0]), (plus.at[1], minus.at[1]), left, own)
    _, _, here = axes()
    for stage in range(4):
        for h in range(2):
            s = (here + (OFFSETS[stage][h] + 4)) % 4
            to[stage][h][...] = sum_ref[h, s] + (relay0, relay1)[h][s]


def relay_kernel(*refs):
    for h in range(2):
        refs[4 + h][...] = refs[h][...] + refs[2 + h][0]


def call(body, outs, args, name, scratch=(), limit=8, cost=(1_000_000, 4_000_000), onto=None, after=()):
    space = {"v": pltpu.VMEM, "h": pltpu.HBM}
    spec = {"v": VSPEC, "h": ASPEC, "a": ASPEC, "s": pl.BlockSpec(memory_space=pltpu.SMEM)}
    vals = [pltpu.with_memory_space_constraint(a, space[kind]) if kind in space else a for a, kind in args]
    in_specs = [spec[kind] for _, kind in args]
    outs = list(outs) if isinstance(outs, (list, tuple)) else [outs]
    aliases = {}
    if onto is not None:
        vals, in_specs, aliases = vals + [onto], in_specs + [ASPEC], {len(vals): 0}
    n_read, n_all, n_out = len(vals), len(vals) + len(after), len(outs)

    def kernel(*refs):
        outs_at = n_all + n_out
        refs[outs_at][...] = jnp.zeros((8, 128), F32)
        body(*refs[:n_read], *refs[n_all:outs_at], *refs[outs_at + 1 :])

    vals, in_specs = vals + list(after), in_specs + [ASPEC] * len(after)
    return pl.pallas_call(
        kernel,
        out_shape=outs + [vm((8, 128))],
        in_specs=in_specs,
        out_specs=[ASPEC if isinstance(o, jax.ShapeDtypeStruct) else VSPEC for o in outs] + [VSPEC],
        scratch_shapes=list(scratch),
        input_output_aliases=aliases,
        compiler_params=pltpu.CompilerParams(vmem_limit_bytes=limit * 2**20),
        cost_estimate=pl.CostEstimate(flops=cost[0], bytes_accessed=cost[1], transcendentals=0),
        name=name,
    )(*vals)


def place(z, y, c):
    return (z % NZ * NY + y % NY) * NC + c % NC


def everywhere():
    return [(z, y, c) for z in range(NZ) for y in range(NY) for c in range(NC)]


def to_other_core(x):
    return lax.ppermute(x, "shard", [(place(z, y, c), place(z, y, c + 1)) for z, y, c in everywhere()])


def along(x, step, second=False):
    pairs = []
    for z, y, c in everywhere():
        to = (z + step, y, c) if (c == 0) != second else (z, y + step, c)
        pairs.append((place(z, y, c), place(*to)))
    return lax.ppermute(x, "shard", pairs)


def swap_grp(x, k):
    return lax.ppermute(x, "grp", [(i, i ^ k) for i in range(NX)])


def other_core(g, stages, r0, rows, after=()):
    n = len(stages)
    shape = (n, 2, 4, rows, HW)
    scratch = [pltpu.VMEM(shape, BF16), pltpu.SemaphoreType.DMA((n, 2, 4))]
    if n == 1:
        body, out = near_conv_kernel, vm(shape)
    else:
        body, out = conv_kernel, jax.ShapeDtypeStruct(shape, F32)
        scratch = scratch + [pltpu.VMEM((SLOTS, rows, HW), F32), pltpu.SemaphoreType.DMA((SLOTS,))]
    body = functools.partial(body, stages, r0, rows)
    w, done = call(body, out, [(g, "h")], f"conv{stages[0]}", scratch, limit=12, after=after)
    got = to_other_core(w)
    return {stage: (got, (i, r0)) for i, stage in enumerate(stages)}, done


class Part:
    def __init__(self, g, r0, rows, got):
        self.g, self.r0, self.rows, self.got = g, r0, rows, got
        self.small = vm((rows, HW))

    def staging(self, *lead):
        shape = lead + (2, 4, self.rows, HW)
        return [pltpu.VMEM(shape, BF16), pltpu.VMEM(shape, F32)]

    def kernel(self, body, at, outs, args, name, scratch, after, kind="a", **kwargs):
        body = functools.partial(body, at, self.r0, self.rows)
        args = [(self.g, "h")] + [(x, kind) for x in args]
        return call(body, outs, args, name, scratch, limit=14, after=after, **kwargs)

    def both(self, out, second):
        return [along(out[0], -1, second), along(out[1], 1, second)]

    def send(self, after=(), **kwargs):
        outs = [vm((2, 4, self.rows, HW))] * 2
        (ra, ia), (rb, ib) = self.got[0], self.got[1]
        scratch = self.staging(2) + [pltpu.VMEM((2, 8, 128), F32), pltpu.SemaphoreType.DMA((2, 3, 2, 4))]
        args, kind = ([ra], "a") if ra is rb else ([ra, rb], "v")
        *out, done = self.kernel(send_kernel, (ia, ib), outs, args, "send", scratch, after, kind, **kwargs)
        self.first = self.both(out, False)
        return done

    def add(self, body, stage, outs, name, after):
        r, at = self.got[stage]
        own, other = self.staging()
        scratch = [own, other, other, pltpu.SemaphoreType.DMA((3, 2, 4))]
        return self.kernel(body, at, outs, [r] + self.first, name, scratch, after)

    def on(self, after=()):
        *out, done = self.add(pass_kernel, 2, [vm((4, self.rows, HW))] * 2, "pass", after)
        self.relay = self.both(out, False)
        return done

    def before(self, after=()):
        self.sums, done = self.add(before_kernel, 3, vm((2, 4, self.rows, HW)), "before", after)
        return done

    def turn(self, after=()):
        outs = [vm((2, self.rows, HW))] * 2 + [self.small] * 4
        *out, done = call(turn_kernel, outs, [(x, "v") for x in [self.sums] + self.relay], "turn", after=after)
        self.first2 = self.both(out, True)
        self.left, self.own = out[2:4], out[4:6]
        return done

    def on2(self, after=()):
        args = [(x, "v") for x in list(self.left) + self.first2]
        *out, done = call(relay_kernel, [self.small] * 2, args, "relay", after=after)
        self.relay2 = self.both(out, True)
        return done

    def terms(self):
        return list(self.own) + self.relay2 + self.first2[::-1]


def split(x):
    high = x.astype(BF16)
    return high, (x - high.astype(F32)).astype(BF16)


def dot(a, b, last=False):
    return lax.dot_general(a, b, (((1,), (1 if last else 0,)), ((), ())), preferred_element_type=F32)


def dot3(x, high, low):
    xh, xl = split(x)
    n = x.shape[0]
    both = dot(jnp.concatenate([xh, xl], axis=0), high)
    return both[:n] + both[n:] + dot(xh, low)


def basis():
    k, n = np.arange(SPAN)[:, None], np.arange(SPAN)[None, :]
    q = np.sqrt(np.where(k == 0, 1.0, 2.0) / SPAN) * np.cos(np.pi * (2 * n + 1) * k / (2 * SPAN))
    return q, np.kron(np.eye(TILE // SPAN), q.T)


def halves_of(m):
    high = m.astype(np.float32).astype(jnp.bfloat16)
    low = (m - high.astype(np.float64)).astype(np.float32).astype(jnp.bfloat16)
    return [jnp.asarray(high), jnp.asarray(low)]


def entries(p, qh_ref, ql_ref):
    block = lax.broadcasted_iota(jnp.int32, (1, 128), 1) // TOPK * SPAN
    hit = lax.broadcasted_iota(jnp.int32, (TILE, 128), 0) == p % SPAN + block
    at = jnp.where(lax.broadcasted_iota(jnp.int32, (SPAN, 128), 0) == p // SPAN, 1.0, 0.0).astype(BF16)
    return jnp.where(hit, 1.0, 0.0), dot(qh_ref[...], at) + dot(ql_ref[...], at)


def own_kernel(p_ref, qh_ref, ql_ref, bt_ref, b_ref, l_ref):
    @pl.loop(0, NA)
    def _(a):
        for t in range(NT):
            hit, l_ref[a, t] = entries(p_ref[a, t : t + 1, :], qh_ref, ql_ref)
            bt_ref[a, t] = hit.astype(BF16)
            b_ref[a, t] = hit.T.astype(BF16)


def tables_kernel(x0, x1, x2, x3, qh_ref, ql_ref, b_ref, l_ref):
    me = position()[0]
    n = NA * NT
    for i, ref in enumerate((x0, x1, x2, x3)):
        place = pl.ds(pl.multiple_of((me ^ i) * 128, 128), 128)
        p = ref[n:, :].astype(jnp.int32)
        block = lax.broadcasted_iota(jnp.int32, (n, 128), 1) // TOPK * SPAN
        cols = jnp.concatenate([p % SPAN + block] * (128 // n), axis=0).astype(F32).T.astype(jnp.int32)
        for k in range(n):
            hit = lax.broadcasted_iota(jnp.int32, (128, TILE), 1) == cols[:, k : k + 1]
            b_ref[k // NT, k % NT, place, :] = jnp.where(hit, 1.0, 0.0).astype(BF16)
            at = lax.broadcasted_iota(jnp.int32, (SPAN, 128), 0) == p[k : k + 1] // SPAN
            at = jnp.where(at, 1.0, 0.0).astype(BF16)
            l_ref[k // NT, k % NT, :, place] = dot(qh_ref[...], at) + dot(ql_ref[...], at)


def values_kernel(r0, rows, m_ref, count_ref, p_ref, dh_ref, dl_ref, bt_ref, l_ref, *refs):
    own, relay, direct, (*before, up_ref, v_ref) = refs[0:2], refs[2:4], refs[4:6], refs[6:]
    for h in range(2):
        got = own[h][...] + relay[h][...] + direct[h][1]
        up_ref[:, pl.ds(h * HW, HW)] = DECAY * m_ref[pl.ds(r0, rows), pl.ds(h * HW, HW)] + got
    live = lax.broadcasted_iota(jnp.int32, (1, 128), 1) % TOPK < count_ref[0]
    a0, n = r0 // SPAN, v_ref.shape[0]
    if before:
        v_ref[: NT * a0, :] = before[0][...]
    for t in range(NT):
        zh, zl = split(dot3(up_ref[:, pl.ds(t * TILE, TILE)], dh_ref[...], dl_ref[...]))
        for i in range(rows // SPAN):
            at = slice(i * SPAN, (i + 1) * SPAN)
            got = dot(jnp.concatenate([zh[at], zl[at]], axis=0), bt_ref[a0 + i, t])
            v = jnp.sum((got[:SPAN] + got[SPAN:]) * l_ref[a0 + i, t], axis=0, keepdims=True)
            row = NT * (a0 + i) + t
            v_ref[row : row + 1, :] = jnp.where(live, v, 0.0)
    if n == 2 * NT * NA:
        for a in range(NA):
            v_ref[NT * (NA + a) : NT * (NA + a + 1), :] = p_ref[a].astype(F32)


def row_fields(a, v_ref, l_ref, b_ref, eh_ref, el_ref):
    got = []
    for t in range(NT):
        high, low = split(l_ref[a, t] * v_ref[NT * a + t : NT * a + t + 1, :])
        both = dot(jnp.concatenate([high, low], axis=0), b_ref[a, t])
        got.append(both[:SPAN] + both[SPAN:])
    return dot3(jnp.concatenate(got, axis=0), eh_ref[...], el_ref[...])


def keep_kernel(up0_ref, up1_ref, v_ref, eh_ref, el_ref, b_ref, l_ref, out_ref, buf, sems):
    copies = []
    for a in range(NA):
        rows = pl.ds(a * SPAN, SPAN)
        got = row_fields(a, v_ref, l_ref, b_ref, eh_ref, el_ref)
        for t in range(NT):
            cols = pl.ds(t * TILE, TILE)
            up_ref, r0 = (up0_ref, 0) if a * SPAN < PARTS[1][0] else (up1_ref, PARTS[1][0])
            buf[rows, cols] = up_ref[pl.ds(a * SPAN - r0, SPAN), cols] - got[t * SPAN : (t + 1) * SPAN]
        copies.append(pltpu.make_async_copy(buf.at[rows], out_ref.at[rows], sems.at[a]))
        copies[-1].start()
    for cp in copies:
        cp.wait()


def update_kernel(v0, v1, v2, v3, eh_ref, el_ref, b_ref, l_ref, out_ref, buf, vals, sems):
    me = position()[0]
    for i, ref in enumerate((v0, v1, v2, v3)):
        vals[:, pl.ds(pl.multiple_of((me ^ i) * 128, 128), 128)] = ref[: NT * NA, :] * (1.0 / NX)
    copies = []
    for a in range(NA):
        rows = pl.ds(a * SPAN, SPAN)
        got = row_fields(a, vals, l_ref, b_ref, eh_ref, el_ref)
        for t in range(NT):
            buf[rows, pl.ds(t * TILE, TILE)] = got[t * SPAN : (t + 1) * SPAN]
        copies.append(pltpu.make_async_copy(buf.at[rows], out_ref.at[rows], sems.at[a]))
        copies[-1].start()
    for cp in copies:
        cp.wait()


def from_groups(x):
    return [x] + [swap_grp(x, k) for k in (1, 2, 3)]


def per_device(grads, momentum, positions, counts):
    g = grads.reshape(NZ, NY, NC, ROWS, COLS)
    q, four = basis()
    dh, dl = halves_of(four)
    eh, el = halves_of(four.T)
    qh, ql = halves_of(q.T)
    places = positions.reshape(NA, NT, 128)
    (a0, a_rows), (b0, b_rows) = PARTS
    got_a, n = other_core(g, (0,), a0, a_rows)
    got, n = other_core(g, (1,), a0, a_rows, [n])
    got_a.update(got)
    got_b, n = other_core(g, (0, 1), b0, b_rows, [n, got_a[0][0]])
    first, last = parts = [Part(g, a0, a_rows, got_a), Part(g, b0, b_rows, got_b)]
    n = first.send([n], cost=AHEAD)
    n = last.send([n])
    got, n = other_core(g, (2, 3), 0, ROWS, [n])
    got_a.update(got)
    got_b.update(got)
    bt, b, l, n = call(
        own_kernel,
        [vm((NA, NT, TILE, 128), BF16), vm((NA, NT, 128, TILE), BF16), vm((NA, NT, SPAN, 128))],
        [(places, "v"), (qh, "v"), (ql, "v")],
        "own",
        cost=AHEAD,
        after=[n] + first.first,
    )
    n = first.on([n])
    n = first.before([n])
    n = last.on([n])
    n = first.turn([n])
    n = last.before([n])
    n = last.turn([n])
    n = first.on2([n])
    n = last.on2([n])
    ups, vs = [], []
    for part in parts:
        n_rows = NT * (part.r0 + part.rows) // SPAN * (2 if part is last else 1)
        up, v, n = call(
            functools.partial(values_kernel, part.r0, part.rows),
            [vm((part.rows, COLS)), vm((n_rows, 128))],
            [(momentum[0], "v"), (counts, "s"), (places, "v"), (dh, "v"), (dl, "v"), (bt, "v"), (l, "v")]
            + [(x, "v") for x in part.terms() + vs],
            "values",
            after=[n],
        )
        ups, vs = ups + [up], [v]
    whole = jax.ShapeDtypeStruct((ROWS, COLS), F32)
    scratch = [pltpu.VMEM((ROWS, COLS), F32), pltpu.SemaphoreType.DMA((NA,))]
    vs = from_groups(v)
    kept, _ = call(keep_kernel, whole, [(x, "v") for x in (*ups, v, eh, el, b, l)], "keep", scratch)
    *tables, _ = call(
        tables_kernel,
        [vm((NA, NT, NX * 128, TILE), BF16), vm((NA, NT, SPAN, NX * 128))],
        [(x, "v") for x in vs + [qh, ql]],
        "tables",
    )
    update, _ = call(
        update_kernel,
        whole,
        [(x, "v") for x in vs + [eh, el] + tables],
        "update",
        [scratch[0], pltpu.VMEM((NT * NA, NX * 128), F32), scratch[1]],
    )
    return kept[None], update


def solution(mesh):
    in_specs = (
        P("grp", "shard", None, None),
        P("grp", "shard", None),
        P("grp", "shard", None, None),
        P("grp"),
    )
    out_specs = (P("grp", "shard", None), P("shard", None))
    return jax.shard_map(
        per_device, mesh=mesh, in_specs=in_specs, out_specs=out_specs, check_vma=False
    )
```

```python
import functools

import jax
import jax.numpy as jnp
import numpy as np
from jax import lax
from jax.experimental import pallas as pl
from jax.experimental.pallas import tpu as pltpu
from jax.sharding import PartitionSpec as P

SPAN = 64
DECAY = 0.999
NZ, NY, NC, NX = 4, 4, 2, 4
ROWS, COLS = 256, 1024
HW = COLS // 2
TOPK = 32
AHEAD = (200_000_000_000, 1_000_000_000)
SLOTS = 8
NA, NT, TILE = ROWS // SPAN, 4, 256
PARTS = ((0, 128), (128, 128))
OFFSETS = ((2, 2), (1, -1), (-1, 1), (0, 0))
F32, BF16 = jnp.float32, jnp.bfloat16


def vm(shape, dtype=F32):
    return pltpu.VMEM(shape, dtype)


VSPEC = pl.BlockSpec(memory_space=pltpu.VMEM)
ASPEC = pl.BlockSpec(memory_space=pl.ANY)


def position():
    s = lax.axis_index("shard")
    return lax.axis_index("grp"), s // (NY * NC), (s // NC) % NY, s % NC


def axes(other=False):
    _, z, y, c = position()
    c = 1 - c if other else c
    return c, jnp.where(c == 0, z, y), jnp.where(c == 0, y, z)


def fetch(g_ref, buf, sems, stage, r0, rows, other):
    core, first, _ = axes(other)
    copies = {}
    for h in range(2):
        mine = (first + (OFFSETS[stage][h] + 4)) % 4
        for s in range(4):
            z, y = jnp.where(core == 0, mine, s), jnp.where(core == 0, s, mine)
            src = g_ref.at[z, y, core, pl.ds(r0, rows), pl.ds(h * HW, HW)]
            copies[h, s] = pltpu.make_async_copy(src, buf.at[h, s], sems.at[h, s])
            copies[h, s].start()
    return copies


def conv_kernel(stages, r0, rows, g_ref, w_ref, buf, sems, wide, wide_sems):
    copies = [fetch(g_ref, buf.at[i], sems.at[i], stage, r0, rows, True) for i, stage in enumerate(stages)]
    out = []
    for i in range(len(stages)):
        for (h, s), cp in copies[i].items():
            cp.wait()
            slot = len(out) % SLOTS
            if len(out) >= SLOTS:
                out[-SLOTS].wait()
            wide[slot] = buf[i, h, s].astype(F32)
            out.append(pltpu.make_async_copy(wide.at[slot], w_ref.at[i, h, s], wide_sems.at[slot]))
            out[-1].start()
    for cp in out[-SLOTS:]:
        cp.wait()


def near_conv_kernel(stages, r0, rows, g_ref, w_ref, buf, sems):
    copies = [fetch(g_ref, buf.at[i], sems.at[i], stage, r0, rows, True) for i, stage in enumerate(stages)]
    for i in range(len(stages)):
        for (h, s), cp in copies[i].items():
            cp.wait()
            w_ref[i, h, s] = buf[i, h, s].astype(F32)


class Terms:
    def __init__(self, stage, r0, rows, g_ref, r_ref, at, messages, staging, near=False):
        (i, first_row), (own, other, more, sems) = at, staging
        self.own, self.other, self.more = own, r_ref.at[i] if near else other, None if messages is None else more
        self.copies = {key: [cp] for key, cp in fetch(g_ref, own, sems.at[0], stage, r0, rows, False).items()}
        for h, s in self.copies:
            src = r_ref.at[i, h, s, pl.ds(r0 - first_row, rows)]
            if not near:
                self.copies[h, s].append(pltpu.make_async_copy(src, other.at[h, s], sems.at[1, h, s]))
            if messages is not None:
                self.copies[h, s].append(pltpu.make_async_copy(messages[h].at[s], more.at[h, s], sems.at[2, h, s]))
            for cp in self.copies[h, s][1:]:
                cp.start()

    def get(self, h, s):
        for cp in self.copies[h, s]:
            cp.wait()
        total = self.own[h, s].astype(F32) + self.other[h, s]
        return total if self.more is None else total + self.more[h, s]


def send_kernel(at, r0, rows, g_ref, *refs):
    (*others, minus, plus), staging, (made, made_sems) = refs[:-6], refs[-6:-2], refs[-2:]
    near = len(others) == 2
    terms = [
        Terms(i, r0, rows, g_ref, others[i % len(others)], at[i], None, [ref.at[i] for ref in staging], near)
        for i in range(2)
    ]
    copies = []
    for i, to in enumerate(((minus, plus), (plus, minus))):
        for h in range(2):
            for s in range(4):
                made[i, h, s] = terms[i].get(h, s)
                copies.append(pltpu.make_async_copy(made.at[i, h, s], to[h].at[i, s], made_sems.at[i, h, s]))
                copies[-1].start()
    for cp in copies:
        cp.wait()


def pass_kernel(at, r0, rows, g_ref, r_ref, minus, plus, *refs):
    terms = Terms(2, r0, rows, g_ref, r_ref, at, (minus.at[0], plus.at[0]), refs[2:])
    for h in range(2):
        for s in range(4):
            refs[h][s] = terms.get(h, s)


def before_kernel(at, r0, rows, g_ref, r_ref, minus, plus, out_ref, *staging):
    terms = Terms(3, r0, rows, g_ref, r_ref, at, (plus.at[1], minus.at[1]), staging)
    for h in range(2):
        for s in range(4):
            out_ref[h, s] = terms.get(h, s)


def turn_kernel(sum_ref, relay0, relay1, *refs):
    (minus, plus), left, own = refs[0:2], refs[2:4], refs[4:6]
    to = ((minus.at[0], plus.at[0]), (plus.at[1], minus.at[1]), left, own)
    _, _, here = axes()
    for stage in range(4):
        for h in range(2):
            s = (here + (OFFSETS[stage][h] + 4)) % 4
            to[stage][h][...] = sum_ref[h, s] + (relay0, relay1)[h][s]


def relay_kernel(*refs):
    for h in range(2):
        refs[4 + h][...] = refs[h][...] + refs[2 + h][0]


def call(body, outs, args, name, scratch=(), limit=8, cost=(1_000_000, 4_000_000), onto=None, after=()):
    space = {"v": pltpu.VMEM, "h": pltpu.HBM}
    spec = {"v": VSPEC, "h": ASPEC, "a": ASPEC, "s": pl.BlockSpec(memory_space=pltpu.SMEM)}
    vals = [pltpu.with_memory_space_constraint(a, space[kind]) if kind in space else a for a, kind in args]
    in_specs = [spec[kind] for _, kind in args]
    outs = list(outs) if isinstance(outs, (list, tuple)) else [outs]
    aliases = {}
    if onto is not None:
        vals, in_specs, aliases = vals + [onto], in_specs + [ASPEC], {len(vals): 0}
    n_read, n_all, n_out = len(vals), len(vals) + len(after), len(outs)

    def kernel(*refs):
        outs_at = n_all + n_out
        refs[outs_at][...] = jnp.zeros((8, 128), F32)
        body(*refs[:n_read], *refs[n_all:outs_at], *refs[outs_at + 1 :])

    vals, in_specs = vals + list(after), in_specs + [ASPEC] * len(after)
    return pl.pallas_call(
        kernel,
        out_shape=outs + [vm((8, 128))],
        in_specs=in_specs,
        out_specs=[ASPEC if isinstance(o, jax.ShapeDtypeStruct) else VSPEC for o in outs] + [VSPEC],
        scratch_shapes=list(scratch),
        input_output_aliases=aliases,
        compiler_params=pltpu.CompilerParams(vmem_limit_bytes=limit * 2**20),
        cost_estimate=pl.CostEstimate(flops=cost[0], bytes_accessed=cost[1], transcendentals=0),
        name=name,
    )(*vals)


def place(z, y, c):
    return (z % NZ * NY + y % NY) * NC + c % NC


def everywhere():
    return [(z, y, c) for z in range(NZ) for y in range(NY) for c in range(NC)]


def to_other_core(x):
    return lax.ppermute(x, "shard", [(place(z, y, c), place(z, y, c + 1)) for z, y, c in everywhere()])


def along(x, step, second=False):
    pairs = []
    for z, y, c in everywhere():
        to = (z + step, y, c) if (c == 0) != second else (z, y + step, c)
        pairs.append((place(z, y, c), place(*to)))
    return lax.ppermute(x, "shard", pairs)


def swap_grp(x, k):
    return lax.ppermute(x, "grp", [(i, i ^ k) for i in range(NX)])


def other_core(g, stages, r0, rows, after=()):
    n = len(stages)
    shape = (n, 2, 4, rows, HW)
    scratch = [pltpu.VMEM(shape, BF16), pltpu.SemaphoreType.DMA((n, 2, 4))]
    if n == 1:
        body, out = near_conv_kernel, vm(shape)
    else:
        body, out = conv_kernel, jax.ShapeDtypeStruct(shape, F32)
        scratch = scratch + [pltpu.VMEM((SLOTS, rows, HW), F32), pltpu.SemaphoreType.DMA((SLOTS,))]
    body = functools.partial(body, stages, r0, rows)
    w, done = call(body, out, [(g, "h")], f"conv{stages[0]}", scratch, limit=12, after=after)
    got = to_other_core(w)
    return {stage: (got, (i, r0)) for i, stage in enumerate(stages)}, done


class Part:
    def __init__(self, g, r0, rows, got):
        self.g, self.r0, self.rows, self.got = g, r0, rows, got
        self.small = vm((rows, HW))

    def staging(self, *lead):
        shape = lead + (2, 4, self.rows, HW)
        return [pltpu.VMEM(shape, BF16), pltpu.VMEM(shape, F32)]

    def kernel(self, body, at, outs, args, name, scratch, after, kind="a", **kwargs):
        body = functools.partial(body, at, self.r0, self.rows)
        args = [(self.g, "h")] + [(x, kind) for x in args]
        return call(body, outs, args, name, scratch, limit=14, after=after, **kwargs)

    def both(self, out, second):
        return [along(out[0], -1, second), along(out[1], 1, second)]

    def send(self, after=(), **kwargs):
        outs = [jax.ShapeDtypeStruct((2, 4, self.rows, HW), F32)] * 2
        (ra, ia), (rb, ib) = self.got[0], self.got[1]
        scratch = self.staging(2)
        scratch += [pltpu.VMEM((2, 8, 128), F32), pltpu.SemaphoreType.DMA((2, 3, 2, 4))]
        scratch += [scratch[1], pltpu.SemaphoreType.DMA((2, 2, 4))]
        args, kind = ([ra], "a") if ra is rb else ([ra, rb], "v")
        *out, done = self.kernel(send_kernel, (ia, ib), outs, args, "send", scratch, after, kind, **kwargs)
        self.first = self.both(out, False)
        return done

    def add(self, body, stage, outs, name, after):
        r, at = self.got[stage]
        own, other = self.staging()
        scratch = [own, other, other, pltpu.SemaphoreType.DMA((3, 2, 4))]
        return self.kernel(body, at, outs, [r] + self.first, name, scratch, after)

    def on(self, after=()):
        *out, done = self.add(pass_kernel, 2, [vm((4, self.rows, HW))] * 2, "pass", after)
        self.relay = self.both(out, False)
        return done

    def before(self, after=()):
        self.sums, done = self.add(before_kernel, 3, vm((2, 4, self.rows, HW)), "before", after)
        return done

    def turn(self, after=()):
        outs = [vm((2, self.rows, HW))] * 2 + [self.small] * 4
        *out, done = call(turn_kernel, outs, [(x, "v") for x in [self.sums] + self.relay], "turn", after=after)
        self.first2 = self.both(out, True)
        self.left, self.own = out[2:4], out[4:6]
        return done

    def on2(self, after=()):
        args = [(x, "v") for x in list(self.left) + self.first2]
        *out, done = call(relay_kernel, [self.small] * 2, args, "relay", after=after)
        self.relay2 = self.both(out, True)
        return done

    def terms(self):
        return list(self.own) + self.relay2 + self.first2[::-1]


def split(x):
    high = x.astype(BF16)
    return high, (x - high.astype(F32)).astype(BF16)


def dot(a, b, last=False):
    return lax.dot_general(a, b, (((1,), (1 if last else 0,)), ((), ())), preferred_element_type=F32)


def dot3(x, high, low):
    xh, xl = split(x)
    n = x.shape[0]
    both = dot(jnp.concatenate([xh, xl], axis=0), high)
    return both[:n] + both[n:] + dot(xh, low)


def basis():
    k, n = np.arange(SPAN)[:, None], np.arange(SPAN)[None, :]
    q = np.sqrt(np.where(k == 0, 1.0, 2.0) / SPAN) * np.cos(np.pi * (2 * n + 1) * k / (2 * SPAN))
    return q, np.kron(np.eye(TILE // SPAN), q.T)


def halves_of(m):
    high = m.astype(np.float32).astype(jnp.bfloat16)
    low = (m - high.astype(np.float64)).astype(np.float32).astype(jnp.bfloat16)
    return [jnp.asarray(high), jnp.asarray(low)]


def entries(p, qh_ref, ql_ref):
    block = lax.broadcasted_iota(jnp.int32, (1, 128), 1) // TOPK * SPAN
    hit = lax.broadcasted_iota(jnp.int32, (TILE, 128), 0) == p % SPAN + block
    at = jnp.where(lax.broadcasted_iota(jnp.int32, (SPAN, 128), 0) == p // SPAN, 1.0, 0.0).astype(BF16)
    return jnp.where(hit, 1.0, 0.0), dot(qh_ref[...], at) + dot(ql_ref[...], at)


def own_kernel(p_ref, qh_ref, ql_ref, bt_ref, b_ref, l_ref):
    @pl.loop(0, NA)
    def _(a):
        for t in range(NT):
            hit, l_ref[a, t] = entries(p_ref[a, t : t + 1, :], qh_ref, ql_ref)
            bt_ref[a, t] = hit.astype(BF16)
            b_ref[a, t] = hit.T.astype(BF16)


def tables_kernel(x0, x1, x2, x3, qh_ref, ql_ref, b_ref, l_ref):
    me = position()[0]
    n = NA * NT
    for i, ref in enumerate((x0, x1, x2, x3)):
        place = pl.ds(pl.multiple_of((me ^ i) * 128, 128), 128)
        p = ref[...]
        block = lax.broadcasted_iota(jnp.int32, (n, 128), 1) // TOPK * SPAN
        cols = jnp.concatenate([p % SPAN + block] * (128 // n), axis=0).astype(F32).T.astype(jnp.int32)
        for k in range(n):
            hit = lax.broadcasted_iota(jnp.int32, (128, TILE), 1) == cols[:, k : k + 1]
            b_ref[k // NT, k % NT, place, :] = jnp.where(hit, 1.0, 0.0).astype(BF16)
            at = lax.broadcasted_iota(jnp.int32, (SPAN, 128), 0) == p[k : k + 1] // SPAN
            at = jnp.where(at, 1.0, 0.0).astype(BF16)
            l_ref[k // NT, k % NT, :, place] = dot(qh_ref[...], at) + dot(ql_ref[...], at)


def copy_kernel(x_ref, o_ref):
    for a in range(NA):
        o_ref[NT * a : NT * (a + 1), :] = x_ref[a]


def values_kernel(r0, rows, m_ref, count_ref, dh_ref, dl_ref, bt_ref, l_ref, *refs):
    own, relay, direct, (*before, up_ref, v_ref) = refs[0:2], refs[2:4], refs[4:6], refs[6:]
    for h in range(2):
        got = own[h][...] + relay[h][...] + direct[h][1]
        up_ref[:, pl.ds(h * HW, HW)] = DECAY * m_ref[pl.ds(r0, rows), pl.ds(h * HW, HW)] + got
    live = lax.broadcasted_iota(jnp.int32, (1, 128), 1) % TOPK < count_ref[0]
    a0 = r0 // SPAN
    if before:
        v_ref[: NT * a0, :] = before[0][...]
    for t in range(NT):
        zh, zl = split(dot3(up_ref[:, pl.ds(t * TILE, TILE)], dh_ref[...], dl_ref[...]))
        for i in range(rows // SPAN):
            at = slice(i * SPAN, (i + 1) * SPAN)
            got = dot(jnp.concatenate([zh[at], zl[at]], axis=0), bt_ref[a0 + i, t])
            v = jnp.sum((got[:SPAN] + got[SPAN:]) * l_ref[a0 + i, t], axis=0, keepdims=True)
            row = NT * (a0 + i) + t
            v_ref[row : row + 1, :] = jnp.where(live, v, 0.0)


def row_fields(a, v_ref, l_ref, b_ref, eh_ref, el_ref):
    got = []
    for t in range(NT):
        high, low = split(l_ref[a, t] * v_ref[NT * a + t : NT * a + t + 1, :])
        both = dot(jnp.concatenate([high, low], axis=0), b_ref[a, t])
        got.append(both[:SPAN] + both[SPAN:])
    return dot3(jnp.concatenate(got, axis=0), eh_ref[...], el_ref[...])


def keep_kernel(up0_ref, up1_ref, v_ref, eh_ref, el_ref, b_ref, l_ref, out_ref, buf, sems):
    copies = []
    for a in range(NA):
        rows = pl.ds(a * SPAN, SPAN)
        got = row_fields(a, v_ref, l_ref, b_ref, eh_ref, el_ref)
        for t in range(NT):
            cols = pl.ds(t * TILE, TILE)
            up_ref, r0 = (up0_ref, 0) if a * SPAN < PARTS[1][0] else (up1_ref, PARTS[1][0])
            buf[rows, cols] = up_ref[pl.ds(a * SPAN - r0, SPAN), cols] - got[t * SPAN : (t + 1) * SPAN]
        copies.append(pltpu.make_async_copy(buf.at[rows], out_ref.at[rows], sems.at[a]))
        copies[-1].start()
    for cp in copies:
        cp.wait()


def update_kernel(v0, v1, v2, v3, eh_ref, el_ref, b_ref, l_ref, out_ref, buf, vals, sems):
    me = position()[0]
    for i, ref in enumerate((v0, v1, v2, v3)):
        vals[:, pl.ds(pl.multiple_of((me ^ i) * 128, 128), 128)] = ref[...] * (1.0 / NX)
    copies = []
    for a in range(NA):
        rows = pl.ds(a * SPAN, SPAN)
        got = row_fields(a, vals, l_ref, b_ref, eh_ref, el_ref)
        for t in range(NT):
            buf[rows, pl.ds(t * TILE, TILE)] = got[t * SPAN : (t + 1) * SPAN]
        copies.append(pltpu.make_async_copy(buf.at[rows], out_ref.at[rows], sems.at[a]))
        copies[-1].start()
    for cp in copies:
        cp.wait()


def from_groups(x):
    return [x] + [swap_grp(x, k) for k in (1, 2, 3)]


def per_device(grads, momentum, positions, counts):
    g = grads.reshape(NZ, NY, NC, ROWS, COLS)
    q, four = basis()
    dh, dl = halves_of(four)
    eh, el = halves_of(four.T)
    qh, ql = halves_of(q.T)
    places = positions.reshape(NA, NT, 128)
    (a0, a_rows), (b0, b_rows) = PARTS
    got_a, n = other_core(g, (0,), a0, a_rows)
    got, n = other_core(g, (1,), a0, a_rows, [n])
    got_a.update(got)
    got_b, n = other_core(g, (0, 1), b0, b_rows, [n, got_a[0][0]])
    first, last = parts = [Part(g, a0, a_rows, got_a), Part(g, b0, b_rows, got_b)]
    n = first.send([n], cost=AHEAD)
    n = last.send([n])
    got, n = other_core(g, (2, 3), 0, ROWS, [n])
    got_a.update(got)
    got_b.update(got)
    spread, n = call(copy_kernel, vm((NT * NA, 128), jnp.int32), [(places, "v")], "places", after=[n])
    *tables, n = call(
        tables_kernel,
        [vm((NA, NT, NX * 128, TILE), BF16), vm((NA, NT, SPAN, NX * 128))],
        [(x, "v") for x in from_groups(spread) + [qh, ql]],
        "tables",
        after=[n],
    )
    bt, b, l, n = call(
        own_kernel,
        [vm((NA, NT, TILE, 128), BF16), vm((NA, NT, 128, TILE), BF16), vm((NA, NT, SPAN, 128))],
        [(places, "v"), (qh, "v"), (ql, "v")],
        "own",
        cost=AHEAD,
        after=[n] + first.first,
    )
    n = first.on([n])
    n = first.before([n])
    n = last.on([n])
    n = first.turn([n])
    n = last.before([n])
    n = last.turn([n])
    n = first.on2([n])
    n = last.on2([n])
    ups, vs = [], []
    for part in parts:
        n_rows = NT * (part.r0 + part.rows) // SPAN
        up, v, n = call(
            functools.partial(values_kernel, part.r0, part.rows),
            [vm((part.rows, COLS)), vm((n_rows, 128))],
            [(momentum[0], "v"), (counts, "s"), (dh, "v"), (dl, "v"), (bt, "v"), (l, "v")]
            + [(x, "v") for x in part.terms() + vs],
            "values",
            after=[n],
        )
        ups, vs = ups + [up], [v]
    whole = jax.ShapeDtypeStruct((ROWS, COLS), F32)
    scratch = [pltpu.VMEM((ROWS, COLS), F32), pltpu.SemaphoreType.DMA((NA,))]
    vs = from_groups(v)
    kept, _ = call(keep_kernel, whole, [(x, "v") for x in (*ups, v, eh, el, b, l)], "keep", scratch)
    update, _ = call(
        update_kernel,
        whole,
        [(x, "v") for x in vs + [eh, el] + tables],
        "update",
        [scratch[0], pltpu.VMEM((NT * NA, NX * 128), F32), scratch[1]],
    )
    return kept[None], update


def solution(mesh):
    in_specs = (
        P("grp", "shard", None, None),
        P("grp", "shard", None),
        P("grp", "shard", None, None),
        P("grp"),
    )
    out_specs = (P("grp", "shard", None), P("shard", None))
    return jax.shard_map(
        per_device, mesh=mesh, in_specs=in_specs, out_specs=out_specs, check_vma=False
    )
```

```python
import functools

import jax
import jax.numpy as jnp
import numpy as np
from jax import lax
from jax.experimental import pallas as pl
from jax.experimental.pallas import tpu as pltpu
from jax.sharding import PartitionSpec as P

SPAN = 64
DECAY = 0.999
NZ, NY, NC, NX = 4, 4, 2, 4
ROWS, COLS = 256, 1024
HW = COLS // 2
TOPK = 32
AHEAD = (200_000_000_000, 1_000_000_000)
SLOTS = 8
NA, NT, TILE = ROWS // SPAN, 4, 256
PARTS = ((0, 128), (128, 128))
OFFSETS = ((2, 2), (1, -1), (-1, 1), (0, 0))
F32, BF16 = jnp.float32, jnp.bfloat16


def vm(shape, dtype=F32):
    return pltpu.VMEM(shape, dtype)


VSPEC = pl.BlockSpec(memory_space=pltpu.VMEM)
ASPEC = pl.BlockSpec(memory_space=pl.ANY)


def position():
    s = lax.axis_index("shard")
    return lax.axis_index("grp"), s // (NY * NC), (s // NC) % NY, s % NC


def axes(other=False):
    _, z, y, c = position()
    c = 1 - c if other else c
    return c, jnp.where(c == 0, z, y), jnp.where(c == 0, y, z)


def fetch(g_ref, buf, sems, stage, r0, rows, other):
    core, first, _ = axes(other)
    copies = {}
    for h in range(2):
        mine = (first + (OFFSETS[stage][h] + 4)) % 4
        for s in range(4):
            z, y = jnp.where(core == 0, mine, s), jnp.where(core == 0, s, mine)
            src = g_ref.at[z, y, core, pl.ds(r0, rows), pl.ds(h * HW, HW)]
            copies[h, s] = pltpu.make_async_copy(src, buf.at[h, s], sems.at[h, s])
            copies[h, s].start()
    return copies


def conv_kernel(stages, r0, rows, g_ref, w_ref, buf, sems, wide, wide_sems):
    copies = [fetch(g_ref, buf.at[i], sems.at[i], stage, r0, rows, True) for i, stage in enumerate(stages)]
    out = []
    for i in range(len(stages)):
        for (h, s), cp in copies[i].items():
            cp.wait()
            slot = len(out) % SLOTS
            if len(out) >= SLOTS:
                out[-SLOTS].wait()
            wide[slot] = buf[i, h, s].astype(F32)
            out.append(pltpu.make_async_copy(wide.at[slot], w_ref.at[i, h, s], wide_sems.at[slot]))
            out[-1].start()
    for cp in out[-SLOTS:]:
        cp.wait()


def gate_kernel(out_ref):
    out_ref[...] = jnp.zeros((8, 128), F32)


def near_conv_kernel(stages, r0, rows, g_ref, w_ref, buf, sems):
    copies = [fetch(g_ref, buf.at[i], sems.at[i], stage, r0, rows, True) for i, stage in enumerate(stages)]
    for i in range(len(stages)):
        for (h, s), cp in copies[i].items():
            cp.wait()
            w_ref[i, h, s] = buf[i, h, s].astype(F32)


class Terms:
    def __init__(self, stage, r0, rows, g_ref, r_ref, at, messages, staging, near=False):
        (i, first_row), (own, other, more, sems) = at, staging
        self.own, self.other, self.more = own, r_ref.at[i] if near else other, None if messages is None else more
        self.copies = {key: [cp] for key, cp in fetch(g_ref, own, sems.at[0], stage, r0, rows, False).items()}
        for h, s in self.copies:
            src = r_ref.at[i, h, s, pl.ds(r0 - first_row, rows)]
            if not near:
                self.copies[h, s].append(pltpu.make_async_copy(src, other.at[h, s], sems.at[1, h, s]))
            if messages is not None:
                self.copies[h, s].append(pltpu.make_async_copy(messages[h].at[s], more.at[h, s], sems.at[2, h, s]))
            for cp in self.copies[h, s][1:]:
                cp.start()

    def get(self, h, s):
        for cp in self.copies[h, s]:
            cp.wait()
        total = self.own[h, s].astype(F32) + self.other[h, s]
        return total if self.more is None else total + self.more[h, s]


def send_kernel(at, r0, rows, g_ref, *refs):
    (*others, minus, plus), staging, (made, made_sems) = refs[:-6], refs[-6:-2], refs[-2:]
    near = len(others) == 2
    terms = [
        Terms(i, r0, rows, g_ref, others[i % len(others)], at[i], None, [ref.at[i] for ref in staging], near)
        for i in range(2)
    ]
    copies = []
    for i, to in enumerate(((minus, plus), (plus, minus))):
        for h in range(2):
            for s in range(4):
                made[i, h, s] = terms[i].get(h, s)
                copies.append(pltpu.make_async_copy(made.at[i, h, s], to[h].at[i, s], made_sems.at[i, h, s]))
                copies[-1].start()
    for cp in copies:
        cp.wait()


def pass_kernel(at, r0, rows, g_ref, r_ref, minus, plus, *refs):
    terms = Terms(2, r0, rows, g_ref, r_ref, at, (minus.at[0], plus.at[0]), refs[2:])
    for h in range(2):
        for s in range(4):
            refs[h][s] = terms.get(h, s)


def before_kernel(at, r0, rows, g_ref, r_ref, minus, plus, out_ref, *staging):
    terms = Terms(3, r0, rows, g_ref, r_ref, at, (plus.at[1], minus.at[1]), staging)
    for h in range(2):
        for s in range(4):
            out_ref[h, s] = terms.get(h, s)


def turn_kernel(sum_ref, relay0, relay1, *refs):
    (minus, plus), left, own = refs[0:2], refs[2:4], refs[4:6]
    to = ((minus.at[0], plus.at[0]), (plus.at[1], minus.at[1]), left, own)
    _, _, here = axes()
    for stage in range(4):
        for h in range(2):
            s = (here + (OFFSETS[stage][h] + 4)) % 4
            to[stage][h][...] = sum_ref[h, s] + (relay0, relay1)[h][s]


def relay_kernel(*refs):
    for h in range(2):
        refs[4 + h][...] = refs[h][...] + refs[2 + h][0]


def call(body, outs, args, name, scratch=(), limit=8, cost=(1_000_000, 4_000_000), onto=None, after=()):
    space = {"v": pltpu.VMEM, "h": pltpu.HBM}
    spec = {"v": VSPEC, "h": ASPEC, "a": ASPEC, "s": pl.BlockSpec(memory_space=pltpu.SMEM)}
    vals = [pltpu.with_memory_space_constraint(a, space[kind]) if kind in space else a for a, kind in args]
    in_specs = [spec[kind] for _, kind in args]
    outs = list(outs) if isinstance(outs, (list, tuple)) else [outs]
    aliases = {}
    if onto is not None:
        vals, in_specs, aliases = vals + [onto], in_specs + [ASPEC], {len(vals): 0}
    n_read, n_all, n_out = len(vals), len(vals) + len(after), len(outs)

    def kernel(*refs):
        outs_at = n_all + n_out
        refs[outs_at][...] = jnp.zeros((8, 128), F32)
        body(*refs[:n_read], *refs[n_all:outs_at], *refs[outs_at + 1 :])

    vals, in_specs = vals + list(after), in_specs + [ASPEC] * len(after)
    return pl.pallas_call(
        kernel,
        out_shape=outs + [vm((8, 128))],
        in_specs=in_specs,
        out_specs=[ASPEC if isinstance(o, jax.ShapeDtypeStruct) else VSPEC for o in outs] + [VSPEC],
        scratch_shapes=list(scratch),
        input_output_aliases=aliases,
        compiler_params=pltpu.CompilerParams(vmem_limit_bytes=limit * 2**20),
        cost_estimate=pl.CostEstimate(flops=cost[0], bytes_accessed=cost[1], transcendentals=0),
        name=name,
    )(*vals)


def place(z, y, c):
    return (z % NZ * NY + y % NY) * NC + c % NC


def everywhere():
    return [(z, y, c) for z in range(NZ) for y in range(NY) for c in range(NC)]


def to_other_core(x):
    return lax.ppermute(x, "shard", [(place(z, y, c), place(z, y, c + 1)) for z, y, c in everywhere()])


def along(x, step, second=False):
    pairs = []
    for z, y, c in everywhere():
        to = (z + step, y, c) if (c == 0) != second else (z, y + step, c)
        pairs.append((place(z, y, c), place(*to)))
    return lax.ppermute(x, "shard", pairs)


def swap_grp(x, k):
    return lax.ppermute(x, "grp", [(i, i ^ k) for i in range(NX)])


def other_core(g, stages, r0, rows, after=()):
    n = len(stages)
    shape = (n, 2, 4, rows, HW)
    scratch = [pltpu.VMEM(shape, BF16), pltpu.SemaphoreType.DMA((n, 2, 4))]
    if n == 1:
        body, out = near_conv_kernel, vm(shape)
    else:
        body, out = conv_kernel, jax.ShapeDtypeStruct(shape, F32)
        scratch = scratch + [pltpu.VMEM((SLOTS, rows, HW), F32), pltpu.SemaphoreType.DMA((SLOTS,))]
    body = functools.partial(body, stages, r0, rows)
    w, done = call(body, out, [(g, "h")], f"conv{stages[0]}", scratch, limit=12, after=after)
    got = to_other_core(w)
    return {stage: (got, (i, r0)) for i, stage in enumerate(stages)}, done


class Part:
    def __init__(self, g, r0, rows, got):
        self.g, self.r0, self.rows, self.got = g, r0, rows, got
        self.small = vm((rows, HW))

    def staging(self, *lead):
        shape = lead + (2, 4, self.rows, HW)
        return [pltpu.VMEM(shape, BF16), pltpu.VMEM(shape, F32)]

    def kernel(self, body, at, outs, args, name, scratch, after, kind="a", **kwargs):
        body = functools.partial(body, at, self.r0, self.rows)
        args = [(self.g, "h")] + [(x, kind) for x in args]
        return call(body, outs, args, name, scratch, limit=14, after=after, **kwargs)

    def both(self, out, second):
        return [along(out[0], -1, second), along(out[1], 1, second)]

    def send(self, after=(), **kwargs):
        outs = [jax.ShapeDtypeStruct((2, 4, self.rows, HW), F32)] * 2
        (ra, ia), (rb, ib) = self.got[0], self.got[1]
        scratch = self.staging(2)
        scratch += [pltpu.VMEM((2, 8, 128), F32), pltpu.SemaphoreType.DMA((2, 3, 2, 4))]
        scratch += [scratch[1], pltpu.SemaphoreType.DMA((2, 2, 4))]
        args, kind = ([ra], "a") if ra is rb else ([ra, rb], "v")
        *out, done = self.kernel(send_kernel, (ia, ib), outs, args, "send", scratch, after, kind, **kwargs)
        self.first = self.both(out, False)
        return done

    def add(self, body, stage, outs, name, after):
        r, at = self.got[stage]
        own, other = self.staging()
        scratch = [own, other, other, pltpu.SemaphoreType.DMA((3, 2, 4))]
        return self.kernel(body, at, outs, [r] + self.first, name, scratch, after)

    def on(self, after=()):
        *out, done = self.add(pass_kernel, 2, [vm((4, self.rows, HW))] * 2, "pass", after)
        self.relay = self.both(out, False)
        return done

    def before(self, after=()):
        self.sums, done = self.add(before_kernel, 3, vm((2, 4, self.rows, HW)), "before", after)
        return done

    def turn(self, after=()):
        outs = [vm((2, self.rows, HW))] * 2 + [self.small] * 4
        *out, done = call(turn_kernel, outs, [(x, "v") for x in [self.sums] + self.relay], "turn", after=after)
        self.first2 = self.both(out, True)
        self.left, self.own = out[2:4], out[4:6]
        return done

    def on2(self, after=()):
        args = [(x, "v") for x in list(self.left) + self.first2]
        *out, done = call(relay_kernel, [self.small] * 2, args, "relay", after=after)
        self.relay2 = self.both(out, True)
        return done

    def terms(self):
        return list(self.own) + self.relay2 + self.first2[::-1]


def split(x):
    high = x.astype(BF16)
    return high, (x - high.astype(F32)).astype(BF16)


def dot(a, b, last=False):
    return lax.dot_general(a, b, (((1,), (1 if last else 0,)), ((), ())), preferred_element_type=F32)


def dot3(x, high, low):
    xh, xl = split(x)
    n = x.shape[0]
    both = dot(jnp.concatenate([xh, xl], axis=0), high)
    return both[:n] + both[n:] + dot(xh, low)


def basis():
    k, n = np.arange(SPAN)[:, None], np.arange(SPAN)[None, :]
    q = np.sqrt(np.where(k == 0, 1.0, 2.0) / SPAN) * np.cos(np.pi * (2 * n + 1) * k / (2 * SPAN))
    return q, np.kron(np.eye(TILE // SPAN), q.T)


def halves_of(m):
    high = m.astype(np.float32).astype(jnp.bfloat16)
    low = (m - high.astype(np.float64)).astype(np.float32).astype(jnp.bfloat16)
    return [jnp.asarray(high), jnp.asarray(low)]


def entries(p, qh_ref, ql_ref):
    block = lax.broadcasted_iota(jnp.int32, (1, 128), 1) // TOPK * SPAN
    hit = lax.broadcasted_iota(jnp.int32, (TILE, 128), 0) == p % SPAN + block
    at = jnp.where(lax.broadcasted_iota(jnp.int32, (SPAN, 128), 0) == p // SPAN, 1.0, 0.0).astype(BF16)
    return jnp.where(hit, 1.0, 0.0), dot(qh_ref[...], at) + dot(ql_ref[...], at)


def own_kernel(p_ref, qh_ref, ql_ref, bt_ref, b_ref, l_ref):
    @pl.loop(0, NA)
    def _(a):
        for t in range(NT):
            hit, l_ref[a, t] = entries(p_ref[a, t : t + 1, :], qh_ref, ql_ref)
            bt_ref[a, t] = hit.astype(BF16)
            b_ref[a, t] = hit.T.astype(BF16)


def tables_kernel(x0, x1, x2, x3, qh_ref, ql_ref, b_ref, l_ref):
    me = position()[0]
    n = NA * NT
    for i, ref in enumerate((x0, x1, x2, x3)):
        place = pl.ds(pl.multiple_of((me ^ i) * 128, 128), 128)
        p = ref[...]
        block = lax.broadcasted_iota(jnp.int32, (n, 128), 1) // TOPK * SPAN
        cols = jnp.concatenate([p % SPAN + block] * (128 // n), axis=0).astype(F32).T.astype(jnp.int32)
        for k in range(n):
            hit = lax.broadcasted_iota(jnp.int32, (128, TILE), 1) == cols[:, k : k + 1]
            b_ref[k // NT, k % NT, place, :] = jnp.where(hit, 1.0, 0.0).astype(BF16)
            at = lax.broadcasted_iota(jnp.int32, (SPAN, 128), 0) == p[k : k + 1] // SPAN
            at = jnp.where(at, 1.0, 0.0).astype(BF16)
            l_ref[k // NT, k % NT, :, place] = dot(qh_ref[...], at) + dot(ql_ref[...], at)


def copy_kernel(x_ref, o_ref):
    for a in range(NA):
        o_ref[NT * a : NT * (a + 1), :] = x_ref[a]


def values_kernel(r0, rows, m_ref, count_ref, dh_ref, dl_ref, bt_ref, l_ref, *refs):
    own, relay, direct, (*before, up_ref, v_ref) = refs[0:2], refs[2:4], refs[4:6], refs[6:]
    for h in range(2):
        got = own[h][...] + relay[h][...] + direct[h][1]
        up_ref[:, pl.ds(h * HW, HW)] = DECAY * m_ref[pl.ds(r0, rows), pl.ds(h * HW, HW)] + got
    live = lax.broadcasted_iota(jnp.int32, (1, 128), 1) % TOPK < count_ref[0]
    a0 = r0 // SPAN
    if before:
        v_ref[: NT * a0, :] = before[0][...]
    for t in range(NT):
        zh, zl = split(dot3(up_ref[:, pl.ds(t * TILE, TILE)], dh_ref[...], dl_ref[...]))
        for i in range(rows // SPAN):
            at = slice(i * SPAN, (i + 1) * SPAN)
            got = dot(jnp.concatenate([zh[at], zl[at]], axis=0), bt_ref[a0 + i, t])
            v = jnp.sum((got[:SPAN] + got[SPAN:]) * l_ref[a0 + i, t], axis=0, keepdims=True)
            row = NT * (a0 + i) + t
            v_ref[row : row + 1, :] = jnp.where(live, v, 0.0)


def row_fields(a, v_ref, l_ref, b_ref, eh_ref, el_ref):
    got = []
    for t in range(NT):
        high, low = split(l_ref[a, t] * v_ref[NT * a + t : NT * a + t + 1, :])
        both = dot(jnp.concatenate([high, low], axis=0), b_ref[a, t])
        got.append(both[:SPAN] + both[SPAN:])
    return dot3(jnp.concatenate(got, axis=0), eh_ref[...], el_ref[...])


def keep_kernel(up0_ref, up1_ref, v_ref, eh_ref, el_ref, b_ref, l_ref, out_ref, buf, sems):
    copies = []
    for a in range(NA):
        rows = pl.ds(a * SPAN, SPAN)
        got = row_fields(a, v_ref, l_ref, b_ref, eh_ref, el_ref)
        for t in range(NT):
            cols = pl.ds(t * TILE, TILE)
            up_ref, r0 = (up0_ref, 0) if a * SPAN < PARTS[1][0] else (up1_ref, PARTS[1][0])
            buf[rows, cols] = up_ref[pl.ds(a * SPAN - r0, SPAN), cols] - got[t * SPAN : (t + 1) * SPAN]
        copies.append(pltpu.make_async_copy(buf.at[rows], out_ref.at[rows], sems.at[a]))
        copies[-1].start()
    for cp in copies:
        cp.wait()


def update_kernel(v0, v1, v2, v3, eh_ref, el_ref, b_ref, l_ref, out_ref, buf, vals, sems):
    me = position()[0]
    for i, ref in enumerate((v0, v1, v2, v3)):
        vals[:, pl.ds(pl.multiple_of((me ^ i) * 128, 128), 128)] = ref[...] * (1.0 / NX)
    copies = []
    for a in range(NA):
        rows = pl.ds(a * SPAN, SPAN)
        got = row_fields(a, vals, l_ref, b_ref, eh_ref, el_ref)
        for t in range(NT):
            buf[rows, pl.ds(t * TILE, TILE)] = got[t * SPAN : (t + 1) * SPAN]
        copies.append(pltpu.make_async_copy(buf.at[rows], out_ref.at[rows], sems.at[a]))
        copies[-1].start()
    for cp in copies:
        cp.wait()


def from_groups(x):
    return [x] + [swap_grp(x, k) for k in (1, 2, 3)]


def per_device(grads, momentum, positions, counts):
    g = grads.reshape(NZ, NY, NC, ROWS, COLS)
    q, four = basis()
    dh, dl = halves_of(four)
    eh, el = halves_of(four.T)
    qh, ql = halves_of(q.T)
    places = positions.reshape(NA, NT, 128)
    (a0, a_rows), (b0, b_rows) = PARTS
    got_a, n = other_core(g, (0,), a0, a_rows)
    got, n = other_core(g, (1,), a0, a_rows, [n])
    got_a.update(got)
    got_b, n = other_core(g, (0, 1), b0, b_rows, [n])
    _, n = call(gate_kernel, vm((8, 128)), [], "gate", after=[n, got_a[0][0]])
    first, last = parts = [Part(g, a0, a_rows, got_a), Part(g, b0, b_rows, got_b)]
    n = first.send([n], cost=AHEAD)
    n = last.send([n])
    got, n = other_core(g, (2, 3), 0, ROWS, [n])
    got_a.update(got)
    got_b.update(got)
    spread, n = call(copy_kernel, vm((NT * NA, 128), jnp.int32), [(places, "v")], "places", after=[n])
    *tables, n = call(
        tables_kernel,
        [vm((NA, NT, NX * 128, TILE), BF16), vm((NA, NT, SPAN, NX * 128))],
        [(x, "v") for x in from_groups(spread) + [qh, ql]],
        "tables",
        after=[n],
    )
    bt, b, l, n = call(
        own_kernel,
        [vm((NA, NT, TILE, 128), BF16), vm((NA, NT, 128, TILE), BF16), vm((NA, NT, SPAN, 128))],
        [(places, "v"), (qh, "v"), (ql, "v")],
        "own",
        cost=AHEAD,
        after=[n] + first.first,
    )
    n = first.on([n])
    n = first.before([n])
    n = last.on([n])
    n = first.turn([n])
    n = last.before([n])
    n = last.turn([n])
    n = first.on2([n])
    n = last.on2([n])
    ups, vs = [], []
    for part in parts:
        n_rows = NT * (part.r0 + part.rows) // SPAN
        up, v, n = call(
            functools.partial(values_kernel, part.r0, part.rows),
            [vm((part.rows, COLS)), vm((n_rows, 128))],
            [(momentum[0], "v"), (counts, "s"), (dh, "v"), (dl, "v"), (bt, "v"), (l, "v")]
            + [(x, "v") for x in part.terms() + vs],
            "values",
            after=[n],
        )
        ups, vs = ups + [up], [v]
    whole = jax.ShapeDtypeStruct((ROWS, COLS), F32)
    scratch = [pltpu.VMEM((ROWS, COLS), F32), pltpu.SemaphoreType.DMA((NA,))]
    vs = from_groups(v)
    kept, _ = call(keep_kernel, whole, [(x, "v") for x in (*ups, v, eh, el, b, l)], "keep", scratch)
    update, _ = call(
        update_kernel,
        whole,
        [(x, "v") for x in vs + [eh, el] + tables],
        "update",
        [scratch[0], pltpu.VMEM((NT * NA, NX * 128), F32), scratch[1]],
    )
    return kept[None], update


def solution(mesh):
    in_specs = (
        P("grp", "shard", None, None),
        P("grp", "shard", None),
        P("grp", "shard", None, None),
        P("grp"),
    )
    out_specs = (P("grp", "shard", None), P("shard", None))
    return jax.shard_map(
        per_device, mesh=mesh, in_specs=in_specs, out_specs=out_specs, check_vma=False
    )
```
